256 devices in a mesh: ctx: 4 (over x_lo, core), vocab: 64 (over z, y, x_hi).
Axes of the slice: x: 4 (x_hi: 2, x_lo: 2; x = x_hi * 2 + x_lo), y: 4, z: 8, core: 2. Of those that a mesh axis runs over, the one named last changes fastest.
Arguments:
- hidden: bfloat16 [256, 2, 5120], P('ctx'), may hold values from -6 to 6
- gain: bfloat16 [5120], replicated, may hold values from 0.5 to 1.5
- head: bfloat16 [5120, 81920], P('ctx', 'vocab'), as said below
- targets: int32 [256, 2], P('ctx'), may hold values from 0 to 81919
- prompt_length: int32 [2], replicated, may hold values from 0 to 255
- reference_mean: float32 [2], replicated, may hold values from -14 to -10
- loss_scale: float32 [], replicated, may hold values from 5120 to 20480
Outputs:
- hidden_grad: bfloat16 [256, 2, 5120], P('ctx', None, 'vocab')
- gain_grad: float32 [5120], P('vocab')
- head_grad: bfloat16 [5120, 81920], P('ctx', 'vocab')
- dpo_loss: float32 [], replicated
The draws below stay inside these ranges and needn't reach their ends.
Inputs may be any that keep to these rules, and one draw needn't show every extreme that they name: `head`: every entry lies within 14 / sqrt(5120) of zero.
All inputs are finite; a program needn't handle non-finite values.
Results may differ from the reference program's by a relative error of at most 0.0057.
Values may be sent and summed in bfloat16 or wider, within the bound.
No kernel may reach another device: no remote copies, remote signals or barrier semaphores. Data moves between devices by JAX's collectives and lax.ppermute only.
A program may use at most 384 MiB of HBM per device.

```python
import math
from functools import partial
import jax
import jax.numpy as jnp
import numpy as np
from jax import lax

D = 5120
TOKENS = 256
VOCAB = 81920


def head_column(base_key, vocab_index):
    column_key = jax.random.fold_in(jax.random.fold_in(base_key, 5), vocab_index)
    return jax.random.truncated_normal(column_key, -4.0, 4.0, (D,), jnp.float32) * (3.0 / math.sqrt(D))


def draw_head(key, part):
    base_key = key
    columns = jax.vmap(partial(head_column, base_key))(jnp.arange(VOCAB))
    return columns.T.astype(jnp.bfloat16)


def draw_hidden(key, part):
    key = jax.random.fold_in(key, 23)
    values = jax.random.truncated_normal(key, -5.0, 5.0, (TOKENS, 2, D), jnp.float32)
    return values.astype(jnp.bfloat16)


def plant(array, key, smallest, top_value):
    index_at = [jax.random.randint(jax.random.fold_in(key, axis), (), 0, length) for axis, length in enumerate(array.shape)]
    longest = array.shape.index(max(array.shape))
    beside = index_at[:longest] + [(index_at[longest] + 1) % array.shape[longest]] + index_at[longest + 1:]
    return array.at[tuple(index_at)].set(smallest).at[tuple(beside)].set(top_value)


def wide_ids(stream_key, extent, amount, lean):
    weights = [min(1 << octave, amount + 1 - (1 << octave)) * (1 << 20) // math.isqrt((1 << octave) ** lean) + 1 for octave in range((amount + 1).bit_length()) if 1 << octave <= amount]
    deviation = 1 + sum(weights) // (1 << 30)
    table = np.cumsum(np.array([max(1, weight // deviation) for weight in weights]))
    ticket = jax.random.randint(jax.random.fold_in(stream_key, 1), extent, 0, int(table[len(weights) - 1]))
    start = jnp.left_shift(1, jnp.searchsorted(jnp.asarray(table, jnp.int32), ticket, side="right").astype(jnp.int32))
    grade = start - 1 + jax.random.randint(jax.random.fold_in(stream_key, 4), extent, 0, 1 << 30) % jnp.minimum(start, amount + 1 - start)
    return jax.random.permutation(jax.random.fold_in(stream_key, 2), amount)[grade].astype(jnp.int32)


def setup_inputs(seed: int = 0) -> dict:
    streams_of = jax.random.split(jax.random.key(seed), 8)
    return {
        "hidden": draw_hidden(jax.random.fold_in(streams_of[7], 71), 0),
        "gain": jnp.clip(1.0 + 0.1 * jax.random.normal(streams_of[1], (D,), jnp.float32), 0.5, 1.5).astype(jnp.bfloat16),
        "head": draw_head(jax.random.fold_in(streams_of[7], 71), 0),
        "targets": plant(wide_ids(streams_of[3], (TOKENS, 2), VOCAB, 2), jax.random.fold_in(streams_of[3], 3), 0, VOCAB - 1).astype(jnp.int32),
        "prompt_length": jax.random.randint(streams_of[4], (2,), 0, TOKENS).astype(jnp.int32),
        "reference_mean": jnp.clip(jax.random.uniform(streams_of[5], (2,), jnp.float32, -14.0, -10.0), -14.0, -10.0),
        "loss_scale": jnp.clip(jnp.exp(jax.random.uniform(streams_of[6], (), jnp.float32, math.log(5120.0), math.log(20480.0))), 5120.0, 20480.0),
    }


EPSILON = 1e-06
BETA = 1.0

def reference(hidden, gain, head, targets, prompt_length, reference_mean, loss_scale):
    hidden_wide = hidden.astype(jnp.float32)
    inv_rms = lax.rsqrt(lax.optimization_barrier(jnp.mean(hidden_wide * hidden_wide, axis=-1, keepdims=True)) + EPSILON)
    unit_rows = hidden_wide * inv_rms
    gain_wide = gain.astype(jnp.float32)
    normed = (unit_rows * gain_wide).astype(jnp.bfloat16)
    flat_rows = normed.reshape(-1, D)
    logits = jnp.dot(flat_rows, head, preferred_element_type=jnp.float32)
    row_top = lax.optimization_barrier(jnp.max(logits, axis=-1, keepdims=True))
    log_norm = row_top[:, 0] + jnp.log(lax.optimization_barrier(jnp.sum(jnp.exp(logits - row_top), axis=-1)))
    flat_targets = targets.reshape(-1).astype(jnp.int32)
    picked = jnp.take_along_axis(logits, flat_targets[:, None], axis=1)[:, 0]
    token_logp = (picked - log_norm).reshape(TOKENS, 2)
    positions = lax.broadcasted_iota(jnp.int32, (TOKENS, 2), 0)
    loss_mask = (positions >= prompt_length[None, :]).astype(jnp.float32)
    seq_sums = lax.optimization_barrier(jnp.sum(loss_mask * token_logp, axis=0))
    seq_counts = lax.optimization_barrier(jnp.sum(loss_mask, axis=0))
    seq_means = seq_sums / seq_counts
    margin = BETA * (seq_means[0] - reference_mean[0] - (seq_means[1] - reference_mean[1]))
    dpo_loss = jax.nn.softplus(-margin)
    sig_pull = BETA * jax.nn.sigmoid(-margin)
    seq_weight = loss_scale * jnp.stack([-sig_pull, sig_pull]) / seq_counts
    row_weight = (seq_weight[None, :] * loss_mask).reshape(-1)
    row_probs = jnp.exp(logits - log_norm[:, None])
    target_hit = lax.broadcasted_iota(jnp.int32, logits.shape, 1) == flat_targets[:, None]
    logit_grad = (row_weight[:, None] * (target_hit.astype(jnp.float32) - row_probs)).astype(jnp.bfloat16)
    head_grad = lax.dot_general(flat_rows, logit_grad, (((0,), (0,)), ((), ())), preferred_element_type=jnp.float32).astype(jnp.bfloat16)
    normed_grad = lax.dot_general(logit_grad, head, (((1,), (1,)), ((), ())), preferred_element_type=jnp.float32).reshape(TOKENS, 2, D)
    gain_grad = lax.optimization_barrier(jnp.sum(normed_grad * unit_rows, axis=(0, 1)))
    upstream = normed_grad * gain_wide
    inner_mean = lax.optimization_barrier(jnp.mean(upstream * unit_rows, axis=-1, keepdims=True))
    hidden_grad = (inv_rms * (upstream - unit_rows * inner_mean)).astype(jnp.bfloat16)
    return (hidden_grad, gain_grad, head_grad, dpo_loss)
```

```python
from functools import partial

import jax
import jax.numpy as jnp
from jax import lax
from jax.experimental import pallas as pl
from jax.experimental.pallas import tpu as pltpu
from jax.sharding import Mesh, PartitionSpec as P

EPSILON = 1e-06
BETA = 1.0
SIZES = {"xl": 2, "co": 2, "z": 8, "y": 4, "xh": 2}
CTX = ("xl", "co")
VOC = ("z", "y", "xh")
F32 = jnp.float32
BF16 = jnp.bfloat16


def core_swap(x):
    return lax.ppermute(x, "co", [(0, 1), (1, 0)])


def chip_swap(x):
    return lax.ppermute(x, "xl", [(0, 1), (1, 0)])


def x_ring(x, cross):
    perm = []
    for xl in range(2):
        for co in range(2):
            for xh in range(2):
                to = (2 * xh + xl + (1 if co else -1)) % 4
                core = 1 - co if cross else co
                perm.append(((xl * 2 + co) * 2 + xh, ((to % 2) * 2 + core) * 2 + to // 2))
    return lax.ppermute(x, ("xl", "co", "xh"), perm)


def to_owner(x):
    perm = []
    for c in range(4):
        for z in range(8):
            for y in range(4):
                for xh in range(2):
                    source = ((c * 8 + z) * 4 + y) * 2 + xh
                    dest = (((y ^ c) * 8 + 2 * c + z // 4) * 4 + z % 4) * 2 + xh
                    perm.append((source, dest))
    return lax.ppermute(x, ("xl", "co", "z", "y", "xh"), perm)


def back_kernel(head_ref, g0, g1, g2, g3, out_ref):
    rows = g0.shape[0]
    for pair, (a, b) in enumerate(((g0, g1), (g2, g3))):
        both = jnp.concatenate([a[...], b[...]], axis=0)
        acc = lax.dot_general(
            head_ref[...], both, (((1,), (1,)), ((), ())), preferred_element_type=F32
        ).astype(BF16)
        out_ref[2 * pair] = acc[:, :rows]
        out_ref[2 * pair + 1] = acc[:, rows:]


def back_blocks(head, gs):
    feats, vocab = head.shape
    rows = gs[0].shape[0]
    block = 256
    whole = pl.BlockSpec((rows, vocab), lambda i: (0, 0))
    return pl.pallas_call(
        back_kernel,
        grid=(feats // block,),
        in_specs=[pl.BlockSpec((block, vocab), lambda i: (i, 0))] + [whole] * 4,
        out_specs=pl.BlockSpec((4, block, rows), lambda i: (0, i, 0)),
        out_shape=jax.ShapeDtypeStruct((4, feats, rows), BF16),
        compiler_params=pltpu.CompilerParams(vmem_limit_bytes=48 * 1024 * 1024),
    )(head, *gs)


def head_kernel(w_ref, n0, n1, n2, n3, g0, g1, g2, g3, out_ref):
    half = n0.shape[0] // 2
    total = None
    for s in range(2):
        rows = slice(s * half, (s + 1) * half)
        n_s = jnp.concatenate([n[rows, :] for n in (n0, n1, n2, n3)], axis=0)
        g_s = jnp.concatenate([g[rows, :] for g in (g0, g1, g2, g3)], axis=0)
        part = w_ref[s] * lax.dot_general(
            n_s, g_s, (((0,), (0,)), ((), ())), preferred_element_type=F32
        )
        total = part if total is None else total + part
    out_ref[...] = total.astype(BF16)


def head_blocks(weight, ns, gs):
    rows, feats = ns[0].shape
    vocab = gs[0].shape[1]
    block = 256
    return pl.pallas_call(
        head_kernel,
        grid=(feats // block,),
        in_specs=[pl.BlockSpec(memory_space=pltpu.SMEM)]
        + [pl.BlockSpec((rows, block), lambda i: (0, i))] * 4
        + [pl.BlockSpec((rows, vocab), lambda i: (0, 0))] * 4,
        out_specs=pl.BlockSpec((block, vocab), lambda i: (i, 0)),
        out_shape=jax.ShapeDtypeStruct((feats, vocab), BF16),
        compiler_params=pltpu.CompilerParams(vmem_limit_bytes=48 * 1024 * 1024),
    )(weight, *ns, *gs)


def on_device(hidden, gain, head, targets, prompt_length, reference_mean, loss_scale):
    tok_dev, seq_pair, model_width = hidden.shape
    feats, vocab_dev = head.shape
    rows = tok_dev * seq_pair
    ctx = lax.axis_index(CTX)
    voc = lax.axis_index(VOC)

    wide = hidden.astype(F32)
    inv_rms = lax.rsqrt(jnp.mean(wide * wide, axis=-1, keepdims=True) + EPSILON)
    gain_wide = gain.astype(F32)
    normed = (wide * inv_rms * gain_wide).astype(BF16)
    normed = normed.transpose(1, 0, 2).reshape(rows, model_width)

    def part(k):
        return lax.dynamic_slice_in_dim(normed, (ctx ^ k) * feats, feats, 1)

    n_own = part(0)
    n_sib = core_swap(part(1))
    n_far = x_ring(part(2), False)
    n_far_sib = x_ring(part(3), True)

    def logits_of(n):
        return jnp.dot(n, head, preferred_element_type=F32)

    far = logits_of(n_far) + core_swap(logits_of(n_far_sib))
    near = logits_of(n_own) + core_swap(logits_of(n_sib))
    logits = near + chip_swap(far)

    flat_targets = targets.T.reshape(rows)
    local_target = flat_targets - voc * vocab_dev
    hit = lax.broadcasted_iota(jnp.int32, (rows, vocab_dev), 1) == local_target[:, None]
    top = jnp.max(logits, axis=-1)
    below = logits - top[:, None]
    exps = jnp.exp(below)
    stats = jnp.stack(
        [
            top,
            jnp.sum(exps, axis=-1),
            jnp.sum(exps * below, axis=-1),
            jnp.sum(jnp.where(hit, logits, 0.0), axis=-1),
        ]
    )
    shards = lax.all_to_all(
        jnp.broadcast_to(stats[None], (64,) + stats.shape), VOC, 0, 0
    )
    tops, sums, dots, picks = shards[:, 0], shards[:, 1], shards[:, 2], shards[:, 3]
    row_top = jnp.max(tops, axis=0)
    shift = tops - row_top
    scale = jnp.exp(shift)
    row_total = jnp.sum(scale * sums, axis=0)
    row_dot = jnp.sum(scale * (dots + sums * shift), axis=0)
    target_logit = jnp.sum(picks, axis=0)
    log_norm = row_top + jnp.log(row_total)

    positions = ctx * tok_dev + lax.broadcasted_iota(jnp.int32, (seq_pair, tok_dev), 1)
    mask = (positions >= prompt_length[:, None]).astype(F32)
    row_mask = mask.reshape(rows)
    grad = (row_mask[:, None] * (hit.astype(F32) - jnp.exp(logits - log_norm[:, None]))).astype(
        BF16
    )
    g_far = chip_swap(grad)
    g_sib = core_swap(grad)
    g_far_sib = core_swap(g_far)
    gs = (grad, g_sib, g_far, g_far_sib)

    token_logp = (target_logit - log_norm).reshape(seq_pair, tok_dev)
    seq_sums = jnp.sum(mask * token_logp, axis=1)
    seq_sums = seq_sums + core_swap(seq_sums)
    seq_sums = seq_sums + chip_swap(seq_sums)
    every = lax.broadcasted_iota(jnp.int32, (seq_pair, 4 * tok_dev), 1)
    seq_counts = jnp.sum((every >= prompt_length[:, None]).astype(F32), axis=1)
    seq_means = seq_sums / seq_counts
    margin = BETA * (seq_means[0] - reference_mean[0] - (seq_means[1] - reference_mean[1]))
    dpo_loss = jax.nn.softplus(-margin)
    sig_pull = BETA * jax.nn.sigmoid(-margin)
    seq_weight = loss_scale * jnp.stack([-sig_pull, sig_pull]) / seq_counts

    back = back_blocks(head, gs)
    head_grad = head_blocks(seq_weight, (n_own, n_sib, n_far, n_far_sib), gs)
    over_y = lax.all_to_all(back, "y", 0, 0)
    part_y = jnp.sum(over_y.astype(F32), axis=0).astype(BF16)
    over_zx = lax.all_to_all(part_y.reshape(16, feats // 16, rows), ("z", "xh"), 0, 0)
    normed_grad = to_owner(jnp.sum(over_zx.astype(F32), axis=0))

    share = feats // 16
    row_weight = jnp.broadcast_to(seq_weight[:, None], (seq_pair, tok_dev)).reshape(rows)
    normed_grad = normed_grad * row_weight
    inner_mean = (
        row_weight * row_mask * (target_logit - row_top - row_dot / row_total) / model_width
    )
    inv_row = inv_rms[:, :, 0].T.reshape(rows)
    gain_own = lax.dynamic_slice_in_dim(gain_wide, voc * share, share, 0)
    mine = lax.dynamic_slice_in_dim(hidden, voc * share, share, 2)
    unit = mine.transpose(2, 1, 0).reshape(share, rows).astype(F32) * inv_row
    hidden_grad = (inv_row * (normed_grad * gain_own[:, None] - unit * inner_mean)).astype(BF16)
    hidden_grad = hidden_grad.reshape(share, seq_pair, tok_dev).transpose(2, 1, 0)
    gain_grad = jnp.sum(normed_grad * unit, axis=1)
    gain_grad = gain_grad + core_swap(gain_grad)
    gain_grad = gain_grad + chip_swap(gain_grad)
    return (hidden_grad, gain_grad, head_grad, dpo_loss)


def solution(mesh):
    fine = Mesh(mesh.devices.reshape(tuple(SIZES.values())), tuple(SIZES))
    in_specs = (P(CTX, None, None), P(), P(CTX, VOC), P(CTX, None), P(), P(), P())
    out_specs = (P(CTX, None, VOC), P(VOC), P(CTX, VOC), P())
    return jax.shard_map(
        on_device, mesh=fine, in_specs=in_specs, out_specs=out_specs, check_vma=False
    )
```

```python
import jax
import jax.numpy as jnp
from jax import lax
from jax.experimental import pallas as pl
from jax.experimental.pallas import tpu as pltpu
from jax.sharding import Mesh, PartitionSpec as P

EPSILON = 1e-06
BETA = 1.0
SIZES = {"xl": 2, "co": 2, "z": 8, "y": 4, "xh": 2}
CTX = ("xl", "co")
VOC = ("z", "y", "xh")
F32 = jnp.float32
BF16 = jnp.bfloat16
F16 = jnp.float16
PARAMS = pltpu.CompilerParams(vmem_limit_bytes=48 * 1024 * 1024)
SMEM = pl.BlockSpec(memory_space=pltpu.SMEM)
VMEM = pl.BlockSpec(memory_space=pltpu.VMEM)


def core_swap(x):
    return lax.ppermute(x, "co", [(0, 1), (1, 0)])


def chip_swap(x):
    return lax.ppermute(x, "xl", [(0, 1), (1, 0)])


def both_swap(x):
    return lax.ppermute(x, CTX, [(0, 3), (3, 0), (1, 2), (2, 1)])


def x_ring(x, cross):
    perm = []
    for xl in range(2):
        for co in range(2):
            for xh in range(2):
                to = (2 * xh + xl + (1 if co else -1)) % 4
                core = 1 - co if cross else co
                perm.append(((xl * 2 + co) * 2 + xh, ((to % 2) * 2 + core) * 2 + to // 2))
    return lax.ppermute(x, ("xl", "co", "xh"), perm)


def cost(flops, nbytes):
    return pl.CostEstimate(flops=flops, bytes_accessed=nbytes, transcendentals=0)


def normed_slice(ctx, k, hidden_ref, gain_ref, inv):
    toks, pair, width = hidden_ref.shape
    feats = width // 4
    at = pl.ds(pl.multiple_of((ctx ^ k) * feats, 128), feats)
    wide = hidden_ref[:, :, at].astype(F32).reshape(toks * pair, feats)
    return (wide * inv * gain_ref[:, at].astype(F32)).astype(BF16)


def far_kernel(ctx_ref, hidden_ref, gain_ref, far_ref, far_sib_ref, inv_ref, keep_ref):
    toks, pair, width = hidden_ref.shape
    feats = width // 4
    total = None
    for f in range(4):
        wide = hidden_ref[:, :, f * feats : (f + 1) * feats].astype(F32).reshape(toks * pair, feats)
        part = jnp.sum(wide * wide, axis=-1, keepdims=True)
        total = part if total is None else total + part
    inv = lax.rsqrt(total / width + EPSILON)
    inv_ref[...] = inv
    keep_ref[...] = inv
    far_ref[...] = normed_slice(ctx_ref[0], 2, hidden_ref, gain_ref, inv)
    far_sib_ref[...] = normed_slice(ctx_ref[0], 3, hidden_ref, gain_ref, inv)


def near_kernel(ctx_ref, hidden_ref, gain_ref, inv_ref, own_ref, sib_ref):
    inv = inv_ref[...]
    own_ref[...] = normed_slice(ctx_ref[0], 0, hidden_ref, gain_ref, inv)
    sib_ref[...] = normed_slice(ctx_ref[0], 1, hidden_ref, gain_ref, inv)


def norm_blocks(ctx, hidden, gain):
    toks, pair, width = hidden.shape
    feats = width // 4
    step = 16
    gain = gain.reshape(1, width)
    inv_spec = pl.BlockSpec((step * pair, 1), lambda i: (i, 0))
    shared = [
        SMEM,
        pl.BlockSpec((step, pair, width), lambda i: (i, 0, 0)),
        pl.BlockSpec((1, width), lambda i: (0, 0)),
    ]
    outs = [pl.BlockSpec((step * pair, feats), lambda i: (i, 0))] * 2
    block = jax.ShapeDtypeStruct((toks * pair, feats), BF16)
    far, far_sib, inv, keep = pl.pallas_call(
        far_kernel,
        grid=(toks // step,),
        in_specs=shared,
        out_specs=outs + [inv_spec] * 2,
        out_shape=[block, block]
        + [jax.ShapeDtypeStruct((toks * pair, 1), F32), pltpu.HBM((toks * pair, 1), F32)],
        compiler_params=PARAMS,
    )(ctx.reshape(1), hidden, gain)
    own, sib = pl.pallas_call(
        near_kernel,
        grid=(toks // step,),
        in_specs=shared + [inv_spec],
        out_specs=outs,
        out_shape=[pltpu.HBM((toks * pair, feats), BF16), block],
        compiler_params=PARAMS,
        cost_estimate=cost(0, 4 * hidden.size),
    )(ctx.reshape(1), hidden, gain, inv)
    return own, sib, far, far_sib, keep


def load_kernel(from_ref, to_ref, sem):
    copy = pltpu.make_async_copy(from_ref, to_ref, sem)
    copy.start()
    copy.wait()


def load(x):
    return pl.pallas_call(
        load_kernel,
        in_specs=[pl.BlockSpec(memory_space=pltpu.HBM)],
        out_specs=VMEM,
        out_shape=pltpu.VMEM(x.shape, x.dtype),
        scratch_shapes=[pltpu.SemaphoreType.DMA],
        compiler_params=PARAMS,
        cost_estimate=cost(1 << 32, 2 * x.size),
    )(x)


def softmax_kernel(near_ref, sib_ref, far_ref, target_ref, exp_ref, own_ref, stats_ref):
    logits = near_ref[...] + sib_ref[...] + far_ref[...].astype(F32)
    hit = lax.broadcasted_iota(jnp.int32, logits.shape, 1) == target_ref[...]
    top = jnp.max(logits, axis=-1, keepdims=True)
    below = logits - top
    exps = jnp.exp(below)
    exp_ref[...] = jnp.where(hit, -1.0, exps).T.astype(BF16)
    columns = [
        top,
        jnp.sum(exps, axis=-1, keepdims=True),
        jnp.sum(exps * below, axis=-1, keepdims=True),
        jnp.sum(jnp.where(hit, logits, 0.0), axis=-1, keepdims=True),
    ]
    rows = logits.shape[0]
    lane = lax.broadcasted_iota(jnp.int32, (rows, 128), 1)
    packed = jnp.zeros((rows, 128), F32)
    for i, column in enumerate(columns):
        packed = jnp.where(lane == i, column, packed)
    lines = packed.T[:8]
    own_ref[...] = lines
    stats_ref[...] = jnp.broadcast_to(lines[None], stats_ref.shape)


def softmax_parts(near, sib, far, targets, shards):
    rows, vocab = near.shape
    return pl.pallas_call(
        softmax_kernel,
        out_shape=[
            jax.ShapeDtypeStruct((vocab, rows), BF16),
            jax.ShapeDtypeStruct((8, rows), F32),
            pltpu.HBM((shards, 8, rows), F32),
        ],
        compiler_params=PARAMS,
    )(near, sib, far, targets)


def combine_kernel(first_ref, length_ref, own_ref, shards_ref, out_ref):
    tops, sums, dots, picks = (shards_ref[:, i, :] for i in range(4))
    rows = tops.shape[1]
    tokens = 2 * rows
    top = jnp.max(tops, axis=0, keepdims=True)
    shift = tops - top
    scale = jnp.exp(shift)
    total = jnp.sum(scale * sums, axis=0, keepdims=True)
    dot = jnp.sum(scale * (dots + sums * shift), axis=0, keepdims=True)
    target = jnp.sum(picks, axis=0, keepdims=True)
    log_norm = top + jnp.log(total)
    lane = lax.broadcasted_iota(jnp.int32, (1, rows), 1)
    second = lane % 2 == 1
    length = jnp.where(second, length_ref[1], length_ref[0])
    mask = (first_ref[0] + lane // 2 >= length).astype(F32)
    counts = [(tokens - length_ref[s]).astype(F32) for s in range(2)]
    ratio = jnp.where(second, jnp.full((1, rows), counts[0]) / counts[1], -1.0) * mask
    logp = mask * (target - log_norm)
    lines = [
        ratio * jnp.exp(own_ref[0:1, :] - log_norm),
        ratio * (1.0 - jnp.exp(target - log_norm)),
        jnp.broadcast_to(jnp.sum(jnp.where(second, 0.0, logp), axis=1, keepdims=True), (1, rows)),
        jnp.broadcast_to(jnp.sum(jnp.where(second, logp, 0.0), axis=1, keepdims=True), (1, rows)),
        ratio * (target - top - dot / total),
    ]
    line = lax.broadcasted_iota(jnp.int32, (8, rows), 0)
    packed = jnp.zeros((8, rows), F32)
    for i, value in enumerate(lines):
        packed = jnp.where(line == i, value, packed)
    out_ref[...] = packed


def combine(first, length, own, shards):
    return pl.pallas_call(
        combine_kernel,
        in_specs=[SMEM, SMEM, pl.BlockSpec(own.shape), pl.BlockSpec(shards.shape)],
        out_shape=jax.ShapeDtypeStruct((8, shards.shape[2]), F32),
        compiler_params=PARAMS,
    )(first.reshape(1), length, own, shards)


def gradient(value, line):
    return jnp.where(value < 0.0, line[1:2, :], -line[0:1, :] * value)


def loss_kernel(length_ref, mean_ref, scale_ref, l0, l1, l2, l3, out_ref):
    rows = l0.shape[1]
    sums = (l0[2:4, :] + l1[2:4, :]) + (l2[2:4, :] + l3[2:4, :])
    counts = [
        jnp.full((1, rows), (2 * rows - length_ref[s]).astype(F32)) for s in range(2)
    ]
    means = [sums[s : s + 1, :] / counts[s] for s in range(2)]
    margin = BETA * (means[0] - mean_ref[0] - (means[1] - mean_ref[1]))
    loss = jnp.maximum(-margin, 0.0) + jnp.log1p(jnp.exp(-jnp.abs(margin)))
    weight = scale_ref[0] * BETA / (1.0 + jnp.exp(margin)) / counts[0]
    line = lax.broadcasted_iota(jnp.int32, out_ref.shape, 0)
    out_ref[...] = jnp.where(line == 0, weight, loss)


def loss_lines(length, mean, scale, lines):
    return pl.pallas_call(
        loss_kernel,
        in_specs=[SMEM] * 3 + [VMEM] * 4,
        out_specs=VMEM,
        out_shape=jax.ShapeDtypeStruct(lines[0].shape, F32),
        compiler_params=PARAMS,
    )(length, mean, scale.reshape(1), *lines)


def stage_kernel(e0, e1, e2, e3, out_ref):
    rows = e0.shape[1]
    for k, ref in enumerate((e0, e1, e2, e3)):
        out_ref[:, k * rows : (k + 1) * rows] = ref[...]


def stage(exps):
    vocab, rows = exps[0].shape
    return pl.pallas_call(
        stage_kernel,
        in_specs=[VMEM] * 4,
        out_specs=VMEM,
        out_shape=pltpu.VMEM((vocab, 4 * rows), BF16),
        compiler_params=PARAMS,
        cost_estimate=cost(0, 16 * vocab * rows),
    )(*exps)


def back_kernel(ctx_ref, head_ref, exps, l0, l1, l2, l3, out_ref, grads):
    rows = l0.shape[1]
    share = out_ref.shape[4]

    @pl.when(pl.program_id(0) == 0)
    def _():
        for k, line in enumerate((l0, l1, l2, l3)):
            at = slice(k * rows, (k + 1) * rows)
            grads[:, at] = gradient(exps[:, at].astype(F32), line).astype(BF16)

    half = pl.ds(pl.multiple_of(pl.program_id(0) * 8 * share, 8 * share), 8 * share)
    acc = jnp.dot(head_ref[half, :], grads[...], preferred_element_type=F32).astype(BF16)
    for k in range(4):
        for y in range(4):
            for b in range(2):
                at = (2 * y + b) * share
                out_ref[ctx_ref[0] ^ k, y, b, 0] = acc[
                    at : at + share, k * rows : (k + 1) * rows
                ]


def back_blocks(ctx, head, exps, lines):
    feats, vocab = head.shape
    rows = lines[0].shape[1]
    share = feats // 16
    return pl.pallas_call(
        back_kernel,
        grid=(2,),
        in_specs=[SMEM] + [VMEM] * 6,
        out_specs=pl.BlockSpec((4, 4, 2, 1, share, rows), lambda i: (0, 0, 0, i, 0, 0)),
        out_shape=pltpu.HBM((4, 4, 2, 2, share, rows), BF16),
        scratch_shapes=[pltpu.VMEM((vocab, 4 * rows), BF16)],
        compiler_params=PARAMS,
        cost_estimate=cost(8 * feats * vocab * rows, 4 * feats * vocab),
    )(ctx.reshape(1), head, exps, *lines)


def sum_kernel(in_ref, out_ref):
    out_ref[0] = jnp.sum(in_ref[0].astype(F32), axis=0).astype(BF16)


def sum_sources(x):
    outer, inner, rest = x.shape[0], x.shape[1], x.shape[2:]
    zeros = (0,) * len(rest)
    return pl.pallas_call(
        sum_kernel,
        grid=(outer,),
        in_specs=[pl.BlockSpec((1, inner) + rest, lambda i: (i, 0) + zeros)],
        out_specs=pl.BlockSpec((1,) + rest, lambda i: (i,) + zeros),
        out_shape=pltpu.HBM((outer,) + rest, BF16),
        compiler_params=PARAMS,
    )(x)


def head_kernel(w_ref, n0, n1, n2, n3, e0, e1, e2, e3, l0, l1, l2, l3, out_ref, grads):
    rows = e0.shape[1]

    @pl.when(pl.program_id(0) == 0)
    def _():
        for k, (exp_ref, line) in enumerate(zip((e0, e1, e2, e3), (l0, l1, l2, l3))):
            grad = gradient(exp_ref[...].astype(F32), line)
            grads[k * rows : (k + 1) * rows, :] = grad.T.astype(BF16)

    n = jnp.concatenate([n0[...], n1[...], n2[...], n3[...]], axis=0)
    acc = lax.dot_general(n, grads[...], (((0,), (0,)), ((), ())), preferred_element_type=F32)
    out_ref[...] = (w_ref[0:1, 0:1] * acc).astype(BF16)


def head_blocks(weight, ns, exps, lines):
    rows, feats = ns[0].shape
    vocab = exps[0].shape[0]
    block = 256
    return pl.pallas_call(
        head_kernel,
        grid=(feats // block,),
        in_specs=[VMEM]
        + [pl.BlockSpec((rows, block), lambda i: (0, i))] * 4
        + [VMEM] * 8,
        out_specs=pl.BlockSpec((block, vocab), lambda i: (i, 0)),
        out_shape=jax.ShapeDtypeStruct((feats, vocab), BF16),
        scratch_shapes=[pltpu.VMEM((4 * rows, vocab), BF16)],
        compiler_params=PARAMS,
        cost_estimate=cost(8 * feats * vocab * rows, 4 * feats * vocab),
    )(weight, *ns, *exps, *lines)


def on_device(hidden, gain, head, targets, prompt_length, reference_mean, loss_scale):
    tok_dev, seq_pair, model_width = hidden.shape
    feats, vocab_dev = head.shape
    rows = tok_dev * seq_pair
    ctx = lax.axis_index(CTX)
    voc = lax.axis_index(VOC)

    n_own, to_sib, to_far, to_far_sib, inv_rms = norm_blocks(ctx, hidden, gain)
    n_far_sib = x_ring(to_far_sib, True)
    n_far = x_ring(to_far, False)
    n_sib = core_swap(to_sib)
    head_near = load(head)

    def logits_of(n):
        return jnp.dot(n, head_near, preferred_element_type=F32)

    n_far, n_far_sib, sib = lax.optimization_barrier((n_far, n_far_sib, logits_of(n_sib)))
    ns = (n_own, n_sib, n_far, n_far_sib)
    far_sib = core_swap(logits_of(n_far_sib).astype(F16))
    far = lax.optimization_barrier(logits_of(n_far))
    far = chip_swap((far + far_sib.astype(F32)).astype(F16))
    local_target = targets.reshape(rows, 1) - voc * vocab_dev
    exps, own, stats = softmax_parts(logits_of(n_own), core_swap(sib), far.astype(F32), local_target, 64)
    shards = lax.all_to_all(stats, VOC, 0, 0)
    e_far = chip_swap(exps)
    e_sib = core_swap(exps)
    e_far_sib = core_swap(e_far)

    every_exp = (exps, e_sib, e_far, e_far_sib)

    own_lines = combine(ctx * tok_dev, prompt_length, own, shards)
    lines = (own_lines, core_swap(own_lines), chip_swap(own_lines), both_swap(own_lines))
    back = back_blocks(ctx, head_near, stage(every_exp), lines)

    loss = loss_lines(prompt_length, reference_mean, loss_scale, lines)
    dpo_loss = loss[1, 0]

    near_sum = lax.all_to_all(
        back.reshape((32,) + back.shape[3:]), ("xl", "co", "y", "xh"), 0, 0
    )
    head_grad = head_blocks(loss, ns, every_exp, lines)
    near_sum, head_grad = lax.optimization_barrier((near_sum, head_grad))
    near_sum = sum_sources(near_sum.reshape((4, 8) + back.shape[3:]))
    over_z = lax.all_to_all(near_sum.reshape((8,) + back.shape[4:]), "z", 0, 0)
    normed_grad = jnp.sum(over_z.astype(F32), axis=0)

    share = feats // 16
    weight = loss[0]
    normed_grad = normed_grad * weight
    inner_mean = weight * own_lines[4] / model_width
    inv_row = inv_rms.reshape(rows)
    gain_own = lax.dynamic_slice_in_dim(gain, voc * share, share, 0).astype(F32)
    mine = lax.dynamic_slice_in_dim(hidden, voc * share, share, 2)
    unit = mine.reshape(rows, share).T.astype(F32) * inv_row
    hidden_grad = (inv_row * (normed_grad * gain_own[:, None] - unit * inner_mean)).astype(BF16)
    hidden_grad = hidden_grad.T.reshape(tok_dev, seq_pair, share)
    gain_grad = jnp.sum(normed_grad * unit, axis=1)
    gain_grad = (gain_grad + core_swap(gain_grad)) + (chip_swap(gain_grad) + both_swap(gain_grad))
    return (hidden_grad, gain_grad, head_grad, dpo_loss)


def solution(mesh):
    fine = Mesh(mesh.devices.reshape(tuple(SIZES.values())), tuple(SIZES))
    in_specs = (P(CTX, None, None), P(), P(CTX, VOC), P(CTX, None), P(), P(), P())
    out_specs = (P(CTX, None, VOC), P(VOC), P(CTX, VOC), P())
    return jax.shard_map(
        on_device, mesh=fine, in_specs=in_specs, out_specs=out_specs, check_vma=False
    )
```
